512 devices in a mesh: pipe: 16 (over x, y_lo), expert: 32 (over z, y_hi, core).
Axes of the slice: x: 4, y: 8 (y_hi: 2, y_lo: 4; y = y_hi * 4 + y_lo), z: 8, core: 2. Of those that a mesh axis runs over, the one named last changes fastest.
Arguments:
- fwd_tokens: bfloat16 [16, 2048, 3584], P('pipe', 'expert'), may hold values from -6 to 6
- bwd_tokens: bfloat16 [16, 2048, 3584], P('pipe', 'expert'), may hold values from -6 to 6
- bwd_cotangent: bfloat16 [16, 2048, 3584], P('pipe', 'expert'), may hold values from -6 to 6
- fwd_routes: int32 [16, 2048, 1], P('pipe', 'expert'), may hold values from 0 to 3; in each aligned block of 64 rows (0 to 63, 64 to 127, ..., all dimensions but the last counted through in order) at most 20 rows name the same one
- bwd_routes: int32 [16, 2048, 1], P('pipe', 'expert'), may hold values from 0 to 3; in each aligned block of 64 rows (0 to 63, 64 to 127, ..., all dimensions but the last counted through in order) at most 20 rows name the same one
- fwd_probs: float32 [16, 2048, 1], P('pipe', 'expert'), may hold values from 0.2 to 1
- bwd_probs: float32 [16, 2048, 1], P('pipe', 'expert'), may hold values from 0.2 to 1
- expert_in: bfloat16 [16, 32, 1792, 256], P('pipe', 'expert'), may hold values from -0.09375 to 0.09375
- expert_out: bfloat16 [16, 32, 256, 1792], P('pipe', 'expert'), may hold values from -0.1875 to 0.1875
Outputs:
- fwd_handoff: bfloat16 [16, 2048, 3584], P('pipe', 'expert')
- bwd_handoff: bfloat16 [16, 2048, 3584], P('pipe', 'expert')
The draws below stay inside these ranges and needn't reach their ends.
Inputs may be any that keep to these rules, and one draw needn't show every extreme that they name: `fwd_routes`: each token names 1 different experts; among the 64 tokens of one device of expert no expert is named more than 20 times, a bound that some block reaches. `bwd_routes`: as for fwd_routes.
All inputs are finite; a program needn't handle non-finite values.
Results may differ from the reference program's by a relative error of at most 0.008.
Values may be sent and summed in bfloat16 or wider, within the bound.
No kernel may reach another device: no remote copies, remote signals or barrier semaphores. Data moves between devices by JAX's collectives and lax.ppermute only.
A program may use at most 64 MiB of HBM per device.

```python
import math
import jax
import jax.numpy as jnp
import numpy as np
from jax import lax

D = 3584
HID = 1024
EXPERTS = 4
TOP = 1
TOK = 64
CAP = 20
HID_PARTS = 4
HID_DEV = 256
TOKENS = 2048
N_PIPE = 16
N_EXPERT = 32


def levels(key, shape, split, least, top_value):
    def one(position, blocks):
        draws = jax.random.uniform(jax.random.fold_in(jax.random.fold_in(key, 6), position), (blocks,), jnp.float32, least / len(split), top_value / len(split))
        return jnp.repeat(jnp.exp(draws), shape[position] // blocks).reshape((-1,) + (1,) * (len(shape) - position - 1))

    factor_of = one(*split[0])
    for cut in split[1:]:
        factor_of = factor_of * one(*cut)
    return factor_of


def routed_block(own_key, own, number, rows, count, top, bound, slope):
    ranking = jax.random.permutation(own_key, count)
    heavy_load, common = load_shares(count, rows * top, bound, slope, True), load_shares(count, rows * top, bound, slope, False)
    places = jnp.arange(count)

    def named(sizes, offset_by):
        used = int((sizes > 0).sum())
        fixed = max(1, used // 4)
        moved = fixed + (places - fixed + offset_by * (used - fixed)) % max(1, count - fixed)
        return jnp.zeros((count,), jnp.int32).at[ranking[jnp.where(places < fixed, places, moved)]].set(jnp.asarray(sizes, jnp.int32))

    sizes = jnp.where(number % 4 == 0, named(heavy_load, number // 4), named(common, number - number // 4 - 1))
    mixed = jax.random.permutation(jax.random.fold_in(own, 3), count)
    donor, receiver = mixed[0:count // 2 * 2:2], mixed[1:count // 2 * 2:2]
    slack = jnp.minimum(sizes[donor] - 1, bound - sizes[receiver]) // 2
    slack = jnp.where((donor == ranking[0]) | (receiver == ranking[0]) | (sizes[receiver] == 0), 0, jnp.maximum(slack, 0))
    moved = jax.random.randint(jax.random.fold_in(own, 4), (count // 2,), 0, 1 << 20) % (slack + 1)
    sizes = sizes.at[donor].add(-moved).at[receiver].add(moved)
    items = jnp.searchsorted(jnp.cumsum(sizes), jnp.arange(rows * top), side="right").astype(jnp.int32)
    listing = items.reshape(top, rows).T
    listing = listing[jax.random.permutation(jax.random.fold_in(own, 1), rows)]
    offset_by = jax.random.randint(jax.random.fold_in(own, 2), (rows, 1), 0, top)
    return jnp.take_along_axis(listing, (jnp.arange(top)[None, :] + offset_by) % top, axis=1)


def load_shares(amount, total, reach, lean, full):
    loads = [(1 << 20) // math.isqrt(rank ** lean) + 1 for rank in range(1, amount + 1)]
    largest = reach if full else min(reach, max(-(-total // amount), total * loads[0] // sum(loads)))
    least = 1 if total - largest >= amount - 1 else 0
    given, rest = [largest] + [least] * (amount - 1), total - largest - least * (amount - 1)
    while rest > 0:
        free = [i for i in range(1, amount) if given[i] < largest] or [i for i in range(1, amount) if given[i] < reach]
        mass, left = sum([loads[i] for i in free]), rest
        for i in free:
            addition = min(reach - given[i], max(1, left * loads[i] // mass), rest)
            given[i] = given[i] + addition
            rest = rest - addition
    return np.array(given)


def noise(stream_key, dims, width, limit, cuts=(), held_as=jnp.bfloat16):
    level = levels(stream_key, dims, cuts, -0.22, 0.18) if cuts else 1.0
    values = jax.random.normal(stream_key, dims, jnp.float32) * width * level
    return jnp.minimum(jnp.maximum(values, -limit), limit).astype(held_as)


def setup_inputs(seed: int = 0) -> dict:
    key_of = jax.random.split(jax.random.key(seed), 10)
    fwd_tokens = noise(key_of[0], (N_PIPE, TOKENS, D), 1.0, 6.0, ((0, 16), (1, 32)))
    bwd_tokens = noise(key_of[1], (N_PIPE, TOKENS, D), 1.0, 6.0, ((0, 16), (1, 32)))
    bwd_cotangent = noise(key_of[2], (N_PIPE, TOKENS, D), 1.0, 6.0, ((0, 16), (1, 32)))
    fwd_routes_keys = jax.random.split(jax.random.fold_in(key_of[3], 1), N_PIPE * TOKENS // TOK)
    fwd_routes_turns = jax.random.permutation(jax.random.fold_in(key_of[3], 3), N_PIPE * TOKENS // TOK)
    fwd_routes = jax.vmap(lambda own, number: routed_block(jax.random.fold_in(key_of[3], 2), own, number, TOK, EXPERTS, TOP, CAP, 2))(fwd_routes_keys, fwd_routes_turns).reshape((N_PIPE, TOKENS, TOP))
    bwd_routes_keys = jax.random.split(jax.random.fold_in(key_of[4], 1), N_PIPE * TOKENS // TOK)
    bwd_routes_turns = jax.random.permutation(jax.random.fold_in(key_of[4], 3), N_PIPE * TOKENS // TOK)
    bwd_routes = jax.vmap(lambda own, number: routed_block(jax.random.fold_in(key_of[4], 2), own, number, TOK, EXPERTS, TOP, CAP, 2))(bwd_routes_keys, bwd_routes_turns).reshape((N_PIPE, TOKENS, TOP))
    fwd_probs = jnp.clip(jnp.exp(math.log(1.0) - 1.609438 * jax.random.uniform(key_of[5], (N_PIPE, TOKENS, TOP), jnp.float32) ** levels(key_of[5], (N_PIPE, TOKENS, TOP), ((0, 16), (1, 32)), -0.2, 0.2)), 0.2, 1.0)
    bwd_probs = jnp.clip(jnp.exp(math.log(1.0) - 1.609438 * jax.random.uniform(key_of[6], (N_PIPE, TOKENS, TOP), jnp.float32) ** levels(key_of[6], (N_PIPE, TOKENS, TOP), ((0, 16), (1, 32)), -0.2, 0.2)), 0.2, 1.0)
    expert_in = noise(key_of[7], (N_PIPE, N_EXPERT, D // 2, HID_DEV), D ** -0.5, 0.09375, ((0, 16), (1, 32)))
    expert_out = noise(key_of[8], (N_PIPE, N_EXPERT, HID_DEV, D // 2), HID ** -0.5, 0.1875, ((0, 16), (1, 32)))
    return dict(fwd_tokens=fwd_tokens, bwd_tokens=bwd_tokens, bwd_cotangent=bwd_cotangent, fwd_routes=fwd_routes, bwd_routes=bwd_routes, fwd_probs=fwd_probs, bwd_probs=bwd_probs, expert_in=expert_in, expert_out=expert_out)


def full_weights(block_in, block_out):
    w_in = block_in.reshape(EXPERTS, HID_PARTS, 2, D // 2, HID_DEV).transpose(0, 2, 3, 1, 4).reshape(EXPERTS, D, HID)
    w_out = block_out.reshape(EXPERTS, HID_PARTS, 2, HID_DEV, D // 2).transpose(0, 1, 3, 2, 4).reshape(EXPERTS, HID, D)
    return w_in, w_out


def route_slots(routes):
    chosen = routes.reshape(N_EXPERT, TOK * TOP).astype(jnp.int32)
    onehot = (chosen[:, :, None] == jnp.arange(EXPERTS, dtype=jnp.int32)[None, None, :]).astype(jnp.int32)
    slots = jnp.sum((jnp.cumsum(onehot, axis=1) - 1) * onehot, axis=2).astype(jnp.int32)
    source = jnp.broadcast_to(jnp.arange(N_EXPERT, dtype=jnp.int32)[:, None], (N_EXPERT, TOK * TOP))
    return chosen.reshape(-1), source.reshape(-1), slots.reshape(-1)


def pack_rows(values, chosen, source, slots):
    spread = jnp.repeat(values, TOP, axis=0)
    buffer = jnp.zeros((EXPERTS, N_EXPERT, CAP, D), values.dtype)
    return buffer.at[chosen, source, slots].set(spread).reshape(EXPERTS, N_EXPERT * CAP, D)


def unpack_rows(buffer, chosen, source, slots, probs):
    picked = buffer.reshape(EXPERTS, N_EXPERT, CAP, D)[chosen, source, slots]
    weighted = picked * probs.reshape(-1)[:, None].astype(jnp.float32)
    return jnp.sum(weighted.reshape(TOKENS, TOP, D), axis=1)


def piece_sum(left, right_full):
    rows = left.shape[1]
    left_parts = left.astype(jnp.float32).reshape(EXPERTS, rows, HID_PARTS, HID_DEV)
    right_parts = right_full.astype(jnp.float32).reshape(EXPERTS, HID_PARTS, HID_DEV, D)
    parts = jnp.einsum('erqh,eqhd->eqrd', left_parts, right_parts).astype(jnp.bfloat16)
    return jnp.sum(parts.astype(jnp.float32), axis=1)


def expert_forward(rows_in, w_in, w_out):
    pre_act = jnp.einsum('erd,edh->erh', rows_in.astype(jnp.float32), w_in.astype(jnp.float32))
    hidden = jax.nn.silu(pre_act).astype(jnp.bfloat16)
    return piece_sum(hidden, w_out)


def expert_backward(rows_in, cot_rows, w_in, w_out):
    pre_act = jnp.einsum('erd,edh->erh', rows_in.astype(jnp.float32), w_in.astype(jnp.float32))
    sigma_act = jax.nn.sigmoid(pre_act)
    d_hidden = jnp.einsum('erd,ehd->erh', cot_rows.astype(jnp.float32), w_out.astype(jnp.float32))
    d_pre = (d_hidden * sigma_act * (1.0 + pre_act * (1.0 - sigma_act))).astype(jnp.bfloat16)
    return piece_sum(d_pre, jnp.swapaxes(w_in, 1, 2))


def one_section(packed):
    fwd_rows, bwd_rows, cot_rows, fwd_route, bwd_route, fwd_prob, bwd_prob, block_in, block_out = packed
    w_in, w_out = full_weights(block_in, block_out)
    chosen, source, slots = route_slots(fwd_route)
    outputs = expert_forward(pack_rows(fwd_rows, chosen, source, slots), w_in, w_out)
    forward_out = (fwd_rows.astype(jnp.float32) + unpack_rows(outputs, chosen, source, slots, fwd_prob)).astype(jnp.bfloat16)
    chosen_b, source_b, slots_b = route_slots(bwd_route)
    grads = expert_backward(pack_rows(bwd_rows, chosen_b, source_b, slots_b), pack_rows(cot_rows, chosen_b, source_b, slots_b), w_in, w_out)
    input_grad = (cot_rows.astype(jnp.float32) + unpack_rows(grads, chosen_b, source_b, slots_b, bwd_prob)).astype(jnp.bfloat16)
    return forward_out, input_grad


def reference(fwd_tokens, bwd_tokens, bwd_cotangent, fwd_routes, bwd_routes, fwd_probs, bwd_probs, expert_in, expert_out):
    forward_out, input_grad = lax.map(one_section, (fwd_tokens, bwd_tokens, bwd_cotangent, fwd_routes, bwd_routes, fwd_probs, bwd_probs, expert_in, expert_out))
    return jnp.roll(forward_out, 1, axis=0), jnp.roll(input_grad, -1, axis=0)
```

```python
import jax
import jax.numpy as jnp
from jax import lax
from jax.experimental import pallas as pl
from jax.experimental.pallas import tpu as pltpu
from jax.sharding import PartitionSpec as P

EXPERTS = 4
CAP = 20
RINGS = 8
F32 = jnp.float32
BF16 = jnp.bfloat16
NN = (((1,), (0,)), ((), ()))
NT = (((1,), (1,)), ((), ()))
TN = (((0,), (0,)), ((), ()))
CORE, PLANE, PAIR = 1, 2, 4
LIMIT = 32 * 1024 * 1024


def dot(left, right, dims=NN):
    return lax.dot_general(left, right, dims, preferred_element_type=F32)


def swap(value, mask, who=None):
    count = lax.axis_size("expert")
    return lax.ppermute(value, "expert", [(i, i ^ mask) for i in range(count) if who is None or who(i)])


def keeps(index):
    return (index >> 2 & 1) == (index & 1)


def moves(index):
    return not keeps(index)


def from_behind(value, steps):
    count = lax.axis_size("pipe")
    return lax.ppermute(value, "pipe", [(i, (i + steps) % count) for i in range(count)])


def ring_exchange(value):
    count = lax.axis_size("expert")
    rings = count // 4
    groups = [[z * 4 + b for z in range(rings)] for b in range(4)]
    cut = value.reshape(rings, -1, value.shape[-1])
    got = lax.all_to_all(cut, "expert", split_axis=0, concat_axis=0, tiled=True, axis_index_groups=groups)
    return got.reshape(value.shape)


def call(body, outs, *args):
    shapes = [jax.ShapeDtypeStruct(s, d) for s, d in outs]
    return pl.pallas_call(
        body,
        out_shape=shapes,
        in_specs=[pl.BlockSpec(memory_space=pltpu.VMEM) for _ in args],
        out_specs=[pl.BlockSpec(memory_space=pltpu.VMEM) for _ in outs],
        compiler_params=pltpu.CompilerParams(vmem_limit_bytes=LIMIT),
    )(*args)


def senders(routes, expert):
    count = routes.shape[1]
    mine = jnp.broadcast_to(routes == expert, (2 * CAP, count))
    upto = lax.broadcasted_iota(jnp.int32, (count, count), 0) <= lax.broadcasted_iota(jnp.int32, (count, count), 1)
    rank = dot(mine.astype(F32).astype(BF16), upto.astype(F32).astype(BF16)).astype(jnp.int32) - 1
    row = lax.broadcasted_iota(jnp.int32, (2 * CAP, count), 0)
    low = mine & (rank == row)
    high = mine & (rank == row - CAP)
    return low.astype(F32).astype(BF16), high.astype(F32).astype(BF16)


def pack_body(routes, low_rows, high_rows, out):
    wide = out.shape[2]
    step = low_rows.shape[1] // 2
    shift = 0 if high_rows.shape[1] == wide * 2 else wide
    for e in range(EXPERTS):
        low, high = senders(routes[...], e)
        for h in range(2):
            part = dot(low, low_rows[:, pl.ds(h * step, wide)])
            part += dot(high, high_rows[:, pl.ds(h * step + shift, wide)])
            out[2 * e + h] = part.astype(BF16)


def halves(rows):
    row = lax.broadcasted_iota(jnp.int32, (rows // 2, rows), 0)
    col = lax.broadcasted_iota(jnp.int32, (rows // 2, rows), 1)
    block = row // CAP
    low = col == row + block * CAP
    high = col == row + block * CAP + CAP
    return low.astype(F32).astype(BF16), high.astype(F32).astype(BF16)


def act_fwd_body(own, other, in1, in2, act, sent):
    rows, wide = own.shape
    low, high = halves(rows)
    for k, ref in enumerate((own, other)):
        a = dot(low, ref[...]).astype(BF16)
        b = dot(high, ref[...]).astype(BF16)
        at = pl.ds(k * (rows // 2), rows // 2)
        for q, w in enumerate((in1, in2)):
            n = w.shape[1]
            part = dot(a, w[pl.ds(0, wide), :]) + dot(b, w[pl.ds(wide, wide), :])
            act[at, pl.ds(q * n, n)] = part
            sent[at, pl.ds(q * n, n)] = part.astype(BF16)


def act_bwd_body(own, other, in1, in2, out1, out2, act, grad, sent_act, sent_grad):
    rows = own.shape[0]
    low, high = halves(rows)
    for k, ref in enumerate((own, other)):
        a = dot(low, ref[...]).astype(BF16)
        b = dot(high, ref[...]).astype(BF16)
        at = pl.ds(k * (rows // 2), rows // 2)
        for q, (wi, wo) in enumerate(((in1, out1), (in2, out2))):
            n = wi.shape[1]
            part = dot(a, wi[...])
            act[at, pl.ds(q * n, n)] = part
            sent_act[at, pl.ds(q * n, n)] = part.astype(BF16)
            part = dot(b, wo[...], NT)
            grad[at, pl.ds(q * n, n)] = part
            sent_grad[at, pl.ds(q * n, n)] = part.astype(BF16)


def out_fwd_body(act, got, out1, out2, own, sent):
    a = act[...] + got[...].astype(F32)
    h = (a * jax.nn.sigmoid(a)).astype(BF16)
    n = out1.shape[0]
    o = dot(h[:, :n], out1[...]) + dot(h[:, n:], out2[...])
    half = own.shape[0]
    own[...] = o[:half]
    sent[...] = o[half:].astype(BF16)


def out_bwd_body(act, got_act, grad, got_grad, in1, in2, own, sent):
    a = act[...] + got_act[...].astype(F32)
    g = grad[...] + got_grad[...].astype(F32)
    s = jax.nn.sigmoid(a)
    r = (g * s * (1.0 + a * (1.0 - s))).astype(BF16)
    n = in1.shape[1]
    u = dot(r[:, :n], in1[...], NT) + dot(r[:, n:], in2[...], NT)
    half = own.shape[0]
    own[...] = u[:half]
    sent[...] = u[half:].astype(BF16)


def finish_body(own, got, out):
    total = (own[...] + got[...].astype(F32)).astype(BF16)
    low, high = halves(out.shape[0])
    wide = out.shape[1]
    out[...] = (dot(low, total[:, :wide], TN) + dot(high, total[:, wide:], TN)).astype(BF16)


def merge_body(routes, probs, rows, got, out):
    wide = got.shape[1]
    block = 2 * CAP
    pairs = [senders(routes[...], e) for e in range(EXPERTS)]
    for h in range(2):
        for q in range(2):
            total = None
            for e in range(EXPERTS):
                part = dot(pairs[e][q], got[pl.ds((2 * e + h) * block, block), :], TN)
                total = part if total is None else total + part
            at = pl.ds((2 * h + q) * wide, wide)
            out[:, at] = (rows[:, at].astype(F32) + probs[...] * total).astype(BF16)


def local(
    fwd_tokens,
    bwd_tokens,
    bwd_cotangent,
    fwd_routes,
    bwd_routes,
    fwd_probs,
    bwd_probs,
    expert_in,
    expert_out,
):
    rings = lax.axis_size("expert") // 4
    index = lax.axis_index("expert")
    keep = (index >> 2 & 1) == (index & 1)
    own_in, own_out = expert_in[0, 0], expert_out[0, 0]
    features, hidden = own_in.shape
    quarter = features // 2
    slots = rings * CAP
    tokens = fwd_tokens.shape[1]
    rows_f, rows_b, rows_c = fwd_tokens[0], bwd_tokens[0], bwd_cotangent[0]
    routes_f, routes_b = fwd_routes.reshape(1, tokens), bwd_routes.reshape(1, tokens)
    probs_f, probs_b = fwd_probs.reshape(tokens, 1), bwd_probs.reshape(tokens, 1)

    z_in, z_out = swap(own_in, PAIR | CORE, moves), swap(own_out, PAIR | CORE, moves)
    y_in, y_out = swap(own_in, PLANE, keeps), swap(own_out, PLANE, keeps)
    v_in, v_out = swap(z_in, PLANE, moves), swap(z_out, PLANE, moves)
    in1, out1 = jnp.where(keep, own_in, z_in), jnp.where(keep, own_out, z_out)
    in2, out2 = jnp.where(keep, y_in, v_in), jnp.where(keep, y_out, v_out)

    (send_f,) = call(pack_body, [((2 * EXPERTS, 2 * CAP, quarter), BF16)], routes_f, rows_f, rows_f)
    (send_b,) = call(pack_body, [((2 * EXPERTS, 2 * CAP, features), BF16)], routes_b, rows_b, rows_c)
    send_f, send_b, z_in, z_out = lax.optimization_barrier((send_f, send_b, z_in, z_out))
    got_f = ring_exchange(send_f).reshape(2 * slots, quarter)
    got_b = ring_exchange(send_b).reshape(2 * slots, features)
    far_f, far_b = swap(got_f, CORE), swap(got_b, CORE)

    pre = (2 * slots, 2 * hidden)
    act_f, sent_f = call(act_fwd_body, [(pre, F32), (pre, BF16)], got_f, far_f, in1, in2)
    act_b, grad_b, sent_a, sent_g = call(
        act_bwd_body, [(pre, F32), (pre, F32), (pre, BF16), (pre, BF16)], got_b, far_b, in1, in2, out1, out2
    )
    back_f, back_a, back_g = swap(sent_f, PAIR), swap(sent_a, PAIR), swap(sent_g, PAIR)
    outs = [((slots, features), F32), ((slots, features), BF16)]
    own_f, cross_f = call(out_fwd_body, outs, act_f, back_f, out1, out2)
    own_b, cross_b = call(out_bwd_body, outs, act_b, back_a, grad_b, back_g, in1, in2)
    cross_f, cross_b = swap(cross_f, CORE), swap(cross_b, CORE)
    shape = [((2 * slots, quarter), BF16)]
    (ret_f,) = call(finish_body, shape, own_f, cross_f)
    (ret_b,) = call(finish_body, shape, own_b, cross_b)
    home_f = ring_exchange(ret_f)
    home_b = ring_exchange(ret_b)
    shape = [((tokens, 2 * features), BF16)]
    (y,) = call(merge_body, shape, routes_f, probs_f, rows_f, home_f)
    (dx,) = call(merge_body, shape, routes_b, probs_b, rows_c, home_b)
    return from_behind(y[None], 1), from_behind(dx[None], -1)


def solution(mesh):
    row = P("pipe", "expert", None)
    block = P("pipe", "expert", None, None)
    return jax.shard_map(
        local,
        mesh=mesh,
        in_specs=(row,) * 7 + (block,) * 2,
        out_specs=(row, row),
        check_vma=False,
    )
```

```python
import jax
import jax.numpy as jnp
from jax import lax
from jax.experimental import pallas as pl
from jax.experimental.pallas import tpu as pltpu
from jax.sharding import PartitionSpec as P

EXPERTS = 4
CAP = 20
RINGS = 8
F32 = jnp.float32
BF16 = jnp.bfloat16
NN = (((1,), (0,)), ((), ()))
NT = (((1,), (1,)), ((), ()))
TN = (((0,), (0,)), ((), ()))
CORE, PLANE, PAIR = 1, 2, 4
LIMIT = 32 * 1024 * 1024


def dot(left, right, dims=NN):
    return lax.dot_general(left, right, dims, preferred_element_type=F32)


def swap(value, mask, other=None):
    count = lax.axis_size("expert")
    masks = [mask if other is None or keeps(i) else other for i in range(count)]
    return lax.ppermute(value, "expert", [(i, i ^ m) for i, m in enumerate(masks) if m])


def keeps(index):
    return (index >> 2 & 1) == (index & 1)


def from_behind(value, steps):
    count = lax.axis_size("pipe")
    return lax.ppermute(value, "pipe", [(i, (i + steps) % count) for i in range(count)])


def ring_exchange(value):
    count = lax.axis_size("expert")
    rings = count // 4
    groups = [[z * 4 + b for z in range(rings)] for b in range(4)]
    cut = value.reshape(rings, -1, value.shape[-1])
    got = lax.all_to_all(cut, "expert", split_axis=0, concat_axis=0, tiled=True, axis_index_groups=groups)
    return got.reshape(value.shape)


def call(body, outs, *args, after=(), flag=None):
    shapes = [jax.ShapeDtypeStruct(s, d) for s, d in outs]
    flags = () if flag is None else (flag,)
    lead = [pl.BlockSpec(memory_space=pltpu.SMEM) for _ in flags]
    lead += [pl.BlockSpec(memory_space=pl.ANY) for _ in after]

    def run(*refs):
        body(*refs[: len(flags)], *refs[len(flags) + len(after) :])

    args = (*flags, *after, *args)
    return pl.pallas_call(
        run,
        out_shape=shapes,
        in_specs=lead + [pl.BlockSpec(memory_space=pltpu.VMEM) for _ in args[len(lead) :]],
        out_specs=[pl.BlockSpec(memory_space=pltpu.VMEM) for _ in outs],
        compiler_params=pltpu.CompilerParams(vmem_limit_bytes=LIMIT),
    )(*args)


def senders(routes, expert):
    count = routes.shape[1]
    mine = jnp.broadcast_to(routes == expert, (2 * CAP, count))
    upto = lax.broadcasted_iota(jnp.int32, (count, count), 0) <= lax.broadcasted_iota(jnp.int32, (count, count), 1)
    rank = dot(mine.astype(F32).astype(BF16), upto.astype(F32).astype(BF16)).astype(jnp.int32) - 1
    row = lax.broadcasted_iota(jnp.int32, (2 * CAP, count), 0)
    low = mine & (rank == row)
    high = mine & (rank == row - CAP)
    return low.astype(F32).astype(BF16), high.astype(F32).astype(BF16)


def pack_body(routes, low_rows, high_rows, out):
    wide = out.shape[2]
    step = low_rows.shape[1] // 2
    shift = 0 if high_rows.shape[1] == wide * 2 else wide
    for e in range(EXPERTS):
        low, high = senders(routes[...], e)
        for h in range(2):
            part = dot(low, low_rows[:, pl.ds(h * step, wide)])
            part += dot(high, high_rows[:, pl.ds(h * step + shift, wide)])
            out[2 * e + h] = part.astype(BF16)


def halves(rows):
    row = lax.broadcasted_iota(jnp.int32, (rows // 2, rows), 0)
    col = lax.broadcasted_iota(jnp.int32, (rows // 2, rows), 1)
    block = row // CAP
    low = col == row + block * CAP
    high = col == row + block * CAP + CAP
    return low.astype(F32).astype(BF16), high.astype(F32).astype(BF16)


def choose(flag, body, *weights):
    keep = flag[0] == 1
    pl.when(keep)(lambda: body(*[w[:-1] for w in weights]))
    pl.when(jnp.logical_not(keep))(lambda: body(*[w[1:] for w in weights]))


def act_fwd_body(flag, own, other, *refs):
    *w_in, act, sent = refs
    rows, wide = own.shape
    low, high = halves(rows)

    def run(pieces):
        for k, ref in enumerate((own, other)):
            a = dot(low, ref[...]).astype(BF16)
            b = dot(high, ref[...]).astype(BF16)
            at = pl.ds(k * (rows // 2), rows // 2)
            for q, w in enumerate(pieces):
                n = w.shape[1]
                part = dot(a, w[pl.ds(0, wide), :]) + dot(b, w[pl.ds(wide, wide), :])
                act[at, pl.ds(q * n, n)] = part
                sent[at, pl.ds(q * n, n)] = part.astype(BF16)

    choose(flag, run, w_in)


def act_bwd_body(flag, own, other, *refs):
    *w_in, act, sent = refs
    low, _ = halves(own.shape[0])
    many = low.shape[0]

    def run(pieces):
        for k, ref in enumerate((own, other)):
            v = dot(low, ref[...]).astype(BF16)
            for q, w in enumerate(pieces):
                at = (pl.ds(k * many, many), pl.ds(q * w.shape[1], w.shape[1]))
                part = dot(v, w[...])
                act[at] = part
                sent[at] = part.astype(BF16)

    choose(flag, run, w_in)


def grad_body(flag, own, other, *refs):
    *w_out, grad, sent = refs
    _, high = halves(own.shape[0])
    many = high.shape[0]

    def run(pieces):
        for k, ref in enumerate((own, other)):
            c = dot(high, ref[...]).astype(BF16)
            for q, w in enumerate(pieces):
                at = (pl.ds(k * many, many), pl.ds(q * w.shape[0], w.shape[0]))
                part = dot(c, w[...], NT)
                grad[at] = part
                sent[at] = part.astype(BF16)

    choose(flag, run, w_out)


def out_body(flag, act_f, got_f, act_b, got_b, grad1, got_grad1, grad2, got_grad2, *refs):
    w_in, w_out = refs[:3], refs[3:6]
    own, sent = refs[6:]
    n = grad1.shape[1]
    half = own.shape[0] // 2
    a = act_f[...] + got_f[...].astype(F32)
    h = (a * jax.nn.sigmoid(a)).astype(BF16)
    r = []
    for q, (grad, got) in enumerate(((grad1, got_grad1), (grad2, got_grad2))):
        at = pl.ds(q * n, n)
        a = act_b[:, at] + got_b[:, at].astype(F32)
        g = grad[...] + got[...].astype(F32)
        s = jax.nn.sigmoid(a)
        r.append((g * s * (1.0 + a * (1.0 - s))).astype(BF16))

    def run(ins, outs):
        o = dot(h[:, :n], outs[0][...]) + dot(h[:, n:], outs[1][...])
        u = dot(r[0], ins[0][...], NT) + dot(r[1], ins[1][...], NT)
        for k, part in enumerate((o, u)):
            at = pl.ds(k * half, half)
            own[at, :] = part[:half]
            sent[at, :] = part[half:].astype(BF16)

    choose(flag, run, w_in, w_out)


def finish_body(own, got, out):
    total = (own[...] + got[...].astype(F32)).astype(BF16)
    low, high = halves(out.shape[0])
    half = total.shape[0] // 2
    out[...] = (dot(low, total[:half], TN) + dot(high, total[half:], TN)).astype(BF16)


def merge_body(routes_f, routes_b, probs_f, probs_b, rows_f, rows_c, got, y, dx):
    wide = got.shape[1]
    block = 2 * CAP
    for k, (routes, probs, rows, out) in enumerate(((routes_f, probs_f, rows_f, y), (routes_b, probs_b, rows_c, dx))):
        pick = [senders(routes[...], e)[k] for e in range(EXPERTS)]
        for h in range(2):
            total = None
            for e in range(EXPERTS):
                part = dot(pick[e], got[pl.ds((2 * e + h) * block, block), :], TN)
                total = part if total is None else total + part
            at = pl.ds(h * wide, wide)
            out[:, at] = (rows[:, at].astype(F32) + probs[...] * total).astype(BF16)


def local(
    fwd_tokens,
    bwd_tokens,
    bwd_cotangent,
    fwd_routes,
    bwd_routes,
    fwd_probs,
    bwd_probs,
    expert_in,
    expert_out,
):
    rings = lax.axis_size("expert") // 4
    index = lax.axis_index("expert")
    keep = (index >> 2 & 1) == (index & 1)
    own_in, own_out = expert_in[0, 0], expert_out[0, 0]
    features, hidden = own_in.shape
    quarter = features // 2
    slots = rings * CAP
    tokens = fwd_tokens.shape[1]
    rows_f, rows_b, rows_c = fwd_tokens[0], bwd_tokens[0], bwd_cotangent[0]
    routes_f, routes_b = fwd_routes.reshape(1, tokens), bwd_routes.reshape(1, tokens)
    probs_f, probs_b = fwd_probs.reshape(tokens, 1), bwd_probs.reshape(tokens, 1)

    m_in = swap(own_in, PLANE, PAIR | CORE)
    m_out = swap(own_out, PLANE, PAIR | CORE)
    v_in, v_out = swap(m_in, 0, PLANE), swap(m_out, 0, PLANE)
    w_in, w_out = (own_in, m_in, v_in), (own_out, m_out, v_out)
    flag = keep.astype(jnp.int32).reshape(1)

    (send_f,) = call(pack_body, [((2 * EXPERTS, 2 * CAP, quarter), BF16)], routes_f, rows_f, rows_f)
    (send_b,) = call(pack_body, [((2 * EXPERTS, 2 * CAP, features), BF16)], routes_b, rows_b, rows_c)
    got_b = ring_exchange(send_b).reshape(2 * slots, features)
    send_f, got_b = lax.optimization_barrier((send_f, got_b))
    got_f = ring_exchange(send_f).reshape(2 * slots, quarter)

    pre, piece = (2 * slots, 2 * hidden), (2 * slots, hidden)
    far_b = swap(got_b, CORE)
    grad1, sent_g1 = call(grad_body, [(piece, F32), (piece, BF16)], got_b, far_b, own_out, m_out, flag=flag)
    back_g1 = swap(sent_g1, PAIR)
    act_b, sent_a = call(act_bwd_body, [(pre, F32), (pre, BF16)], got_b, far_b, *w_in, flag=flag)
    back_a = swap(sent_a, PAIR)
    far_f = swap(got_f, CORE)
    act_f, sent_f = call(act_fwd_body, [(pre, F32), (pre, BF16)], got_f, far_f, *w_in, flag=flag)
    back_f = swap(sent_f, PAIR)
    v_out, sent_f, sent_a, back_g1 = lax.optimization_barrier((v_out, sent_f, sent_a, back_g1))
    grad2, sent_g2 = call(grad_body, [(piece, F32), (piece, BF16)], got_b, far_b, m_out, v_out, flag=flag)
    back_g2 = swap(sent_g2, PAIR)
    own, cross = call(
        out_body,
        [((2 * slots, features), F32), ((2 * slots, features), BF16)],
        *(act_f, back_f, act_b, back_a, grad1, back_g1, grad2, back_g2, *w_in, *w_out),
        flag=flag,
    )
    (ret,) = call(finish_body, [((2 * slots, features), BF16)], own, swap(cross, CORE))
    home = ring_exchange(ret)
    shape = (tokens, 2 * features)
    y, dx = call(
        merge_body, [(shape, BF16), (shape, BF16)], routes_f, routes_b, probs_f, probs_b, rows_f, rows_c, home
    )
    return from_behind(y[None], 1), from_behind(dx[None], -1)


def solution(mesh):
    row = P("pipe", "expert", None)
    block = P("pipe", "expert", None, None)
    return jax.shard_map(
        local,
        mesh=mesh,
        in_specs=(row,) * 7 + (block,) * 2,
        out_specs=(row, row),
        check_vma=False,
    )
```

```python
import jax
import jax.numpy as jnp
from jax import lax
from jax.experimental import pallas as pl
from jax.experimental.pallas import tpu as pltpu
from jax.sharding import PartitionSpec as P

EXPERTS = 4
CAP = 20
LANES = 128
F32 = jnp.float32
BF16 = jnp.bfloat16
NN = (((1,), (0,)), ((), ()))
NT = (((1,), (1,)), ((), ()))
TN = (((0,), (0,)), ((), ()))
CORE, PLANE, PAIR = 1, 2, 4
LIMIT = 32 * 1024 * 1024


def dot(left, right, dims=NN):
    return lax.dot_general(left, right, dims, preferred_element_type=F32)


def swap(value, mask, other=None):
    count = lax.axis_size("expert")
    masks = [mask if other is None or keeps(i) else other for i in range(count)]
    return lax.ppermute(value, "expert", [(i, i ^ m) for i, m in enumerate(masks) if m])


def keeps(index):
    return (index >> 2 & 1) == (index & 1)


def from_behind(value, steps):
    count = lax.axis_size("pipe")
    return lax.ppermute(value, "pipe", [(i, (i + steps) % count) for i in range(count)])


def ring_exchange(value):
    count = lax.axis_size("expert")
    rings = count // 4
    groups = [[z * 4 + b for z in range(rings)] for b in range(4)]
    cut = value.reshape(rings, -1, value.shape[-1])
    got = lax.all_to_all(cut, "expert", split_axis=0, concat_axis=0, tiled=True, axis_index_groups=groups)
    return got.reshape(value.shape)


def call(body, outs, *args, after=(), flag=None):
    shapes = [jax.ShapeDtypeStruct(s, d) for s, d in outs]
    flags = () if flag is None else (flag,)
    lead = [pl.BlockSpec(memory_space=pltpu.SMEM) for _ in flags]
    lead += [pl.BlockSpec(memory_space=pl.ANY) for _ in after]

    def run(*refs):
        body(*refs[: len(flags)], *refs[len(flags) + len(after) :])

    args = (*flags, *after, *args)
    return pl.pallas_call(
        run,
        out_shape=shapes,
        in_specs=lead + [pl.BlockSpec(memory_space=pltpu.VMEM) for _ in args[len(lead) :]],
        out_specs=[pl.BlockSpec(memory_space=pltpu.VMEM) for _ in outs],
        compiler_params=pltpu.CompilerParams(vmem_limit_bytes=LIMIT),
    )(*args)


def gate(held, *after):
    return pl.pallas_call(
        lambda *refs: None,
        out_shape=jax.ShapeDtypeStruct(held.shape, held.dtype),
        in_specs=[pl.BlockSpec(memory_space=pl.ANY) for _ in (held, *after)],
        out_specs=pl.BlockSpec(memory_space=pl.ANY),
        input_output_aliases={0: 0},
        cost_estimate=pl.CostEstimate(flops=10**11, bytes_accessed=10**9, transcendentals=0),
    )(held, *after)


def senders(routes, expert):
    count = routes.shape[1]
    mine = jnp.broadcast_to(routes == expert, (2 * CAP, count))
    upto = lax.broadcasted_iota(jnp.int32, (count, count), 0) <= lax.broadcasted_iota(jnp.int32, (count, count), 1)
    rank = dot(mine.astype(F32).astype(BF16), upto.astype(F32).astype(BF16)).astype(jnp.int32) - 1
    row = lax.broadcasted_iota(jnp.int32, (2 * CAP, count), 0)
    low = mine & (rank == row)
    high = mine & (rank == row - CAP)
    return low.astype(F32).astype(BF16), high.astype(F32).astype(BF16)


def pack_fwd_body(routes, rows, out):
    wide = out.shape[2]
    for e in range(EXPERTS):
        low, high = senders(routes[...], e)
        for h in range(2):
            first, second = pl.ds(2 * h * wide, wide), pl.ds((2 * h + 1) * wide, wide)
            out[2 * e + h] = (dot(low, rows[:, first]) + dot(high, rows[:, second])).astype(BF16)


def pack_bwd_body(routes, probs, rows, cots, out):
    wide = out.shape[2] - LANES
    lane = lax.broadcasted_iota(jnp.int32, (rows.shape[0], LANES), 1)
    rest = jnp.broadcast_to(probs[...], lane.shape)
    weight = jnp.zeros(lane.shape, F32)
    for k in range(3):
        part = rest.astype(BF16).astype(F32)
        weight = jnp.where(lane == k, part, weight)
        rest = rest - part
    weight = weight.astype(BF16)
    for e in range(EXPERTS):
        low, high = senders(routes[...], e)
        tail = dot(low, weight).astype(BF16)
        for h in range(2):
            at = pl.ds(h * wide, wide)
            out[2 * e + h, :, pl.ds(0, wide)] = (dot(low, rows[:, at]) + dot(high, cots[:, at])).astype(BF16)
            out[2 * e + h, :, pl.ds(wide, LANES)] = tail


def halves(rows):
    row = lax.broadcasted_iota(jnp.int32, (rows // 2, rows), 0)
    col = lax.broadcasted_iota(jnp.int32, (rows // 2, rows), 1)
    block = row // CAP
    low = col == row + block * CAP
    high = col == row + block * CAP + CAP
    return low.astype(F32).astype(BF16), high.astype(F32).astype(BF16)


def choose(flag, body, *weights):
    keep = flag[0] == 1
    pl.when(keep)(lambda: body(*[w[:-1] for w in weights]))
    pl.when(jnp.logical_not(keep))(lambda: body(*[w[1:] for w in weights]))


def act_fwd_body(flag, own, other, *refs):
    *w_in, act, sent = refs
    rows, wide = own.shape
    low, high = halves(rows)

    def run(pieces):
        for k, ref in enumerate((own, other)):
            a = dot(low, ref[...]).astype(BF16)
            b = dot(high, ref[...]).astype(BF16)
            at = pl.ds(k * (rows // 2), rows // 2)
            for q, w in enumerate(pieces):
                n = w.shape[1]
                part = dot(a, w[pl.ds(0, wide), :]) + dot(b, w[pl.ds(wide, wide), :])
                act[at, pl.ds(q * n, n)] = part
                sent[at, pl.ds(q * n, n)] = part.astype(BF16)

    choose(flag, run, w_in)


def act_bwd_body(flag, own, other, *refs):
    *w_in, act, sent = refs
    low, _ = halves(own.shape[0])
    many = low.shape[0]

    def run(pieces):
        for k, ref in enumerate((own, other)):
            v = dot(low, ref[:, : pieces[0].shape[0]]).astype(BF16)
            for q, w in enumerate(pieces):
                at = (pl.ds(k * many, many), pl.ds(q * w.shape[1], w.shape[1]))
                part = dot(v, w[...])
                act[at] = part
                sent[at] = part.astype(BF16)

    choose(flag, run, w_in)


def grad_body(flag, own, other, *refs):
    *w_out, grad, sent = refs
    _, high = halves(own.shape[0])
    many = high.shape[0]

    def run(pieces):
        for k, ref in enumerate((own, other)):
            c = dot(high, ref[:, : pieces[0].shape[1]]).astype(BF16)
            for q, w in enumerate(pieces):
                at = (pl.ds(k * many, many), pl.ds(q * w.shape[0], w.shape[0]))
                part = dot(c, w[...], NT)
                grad[at] = part
                sent[at] = part.astype(BF16)

    choose(flag, run, w_out)


def out_body(flag, act_f, got_f, act_b, got_b, grad1, got_grad1, grad2, got_grad2, *refs):
    w_in, w_out = refs[:3], refs[3:6]
    own, sent = refs[6:]
    n = grad1.shape[1]
    half = own.shape[0] // 2
    a = act_f[...] + got_f[...].astype(F32)
    h = (a * jax.nn.sigmoid(a)).astype(BF16)
    r = []
    for q, (grad, got) in enumerate(((grad1, got_grad1), (grad2, got_grad2))):
        at = pl.ds(q * n, n)
        a = act_b[:, at] + got_b[:, at].astype(F32)
        g = grad[...] + got[...].astype(F32)
        s = jax.nn.sigmoid(a)
        r.append((g * s * (1.0 + a * (1.0 - s))).astype(BF16))

    def run(ins, outs):
        o = dot(h[:, :n], outs[0][...]) + dot(h[:, n:], outs[1][...])
        u = dot(r[0], ins[0][...], NT) + dot(r[1], ins[1][...], NT)
        for k, part in enumerate((o, u)):
            at = pl.ds(k * half, half)
            own[at, :] = part[:half]
            sent[at, :] = part[half:].astype(BF16)

    choose(flag, run, w_in, w_out)


def finish_body(own, got, sent, out_f, out_b):
    low, high = halves(out_f.shape[0])
    wide = out_f.shape[1]
    half = own.shape[0] // 2
    total = own[...] + got[...].astype(F32)
    weight = jnp.sum(dot(low, sent[:, 2 * wide :]), axis=1, keepdims=True)
    ready = (dot(high, sent[:, : 2 * wide]) + weight * total[half:]).astype(BF16)
    for rows, out in ((total[:half].astype(BF16), out_f), (ready, out_b)):
        out[...] = (dot(low, rows[:, :wide], TN) + dot(high, rows[:, wide:], TN)).astype(BF16)


def homing(routes, got, place):
    wide = got.shape[1]
    block = 2 * CAP
    picks = [senders(routes[...], e) for e in range(EXPERTS)]
    for h in range(2):
        for q in range(2):
            total = None
            for e in range(EXPERTS):
                part = dot(picks[e][q], got[pl.ds((2 * e + h) * block, block), :], TN)
                total = part if total is None else total + part
            place(pl.ds((2 * h + q) * wide, wide), total)


def merge_fwd_body(routes, probs, rows, got, out):
    def place(at, total):
        out[:, at] = (rows[:, at].astype(F32) + probs[...] * total).astype(BF16)

    homing(routes, got, place)


def merge_bwd_body(routes, got, out):
    def place(at, total):
        out[:, at] = total.astype(BF16)

    homing(routes, got, place)


def local(
    fwd_tokens,
    bwd_tokens,
    bwd_cotangent,
    fwd_routes,
    bwd_routes,
    fwd_probs,
    bwd_probs,
    expert_in,
    expert_out,
):
    rings = lax.axis_size("expert") // 4
    index = lax.axis_index("expert")
    keep = (index >> 2 & 1) == (index & 1)
    own_in, own_out = expert_in[0, 0], expert_out[0, 0]
    features, hidden = own_in.shape
    quarter = features // 2
    slots = rings * CAP
    tokens = fwd_tokens.shape[1]
    rows_f, rows_b, rows_c = fwd_tokens[0], bwd_tokens[0], bwd_cotangent[0]
    routes_f, routes_b = fwd_routes.reshape(1, tokens), bwd_routes.reshape(1, tokens)
    probs_f, probs_b = fwd_probs.reshape(tokens, 1), bwd_probs.reshape(tokens, 1)

    m_in = swap(own_in, PLANE, PAIR | CORE)
    m_out = swap(own_out, PLANE, PAIR | CORE)
    v_in = swap(m_in, 0, PLANE)
    early_out, v_in = lax.optimization_barrier((m_out, v_in))
    v_out = swap(early_out, 0, PLANE)
    w_in, w_out = (own_in, m_in, v_in), (own_out, m_out, v_out)
    flag = keep.astype(jnp.int32).reshape(1)

    (send_f,) = call(pack_fwd_body, [((2 * EXPERTS, 2 * CAP, quarter), BF16)], routes_f, rows_f)
    (send_b,) = call(
        pack_bwd_body, [((2 * EXPERTS, 2 * CAP, features + LANES), BF16)], routes_b, probs_b, rows_b, rows_c
    )
    got_b = ring_exchange(send_b).reshape(2 * slots, features + LANES)
    send_f, got_b = lax.optimization_barrier((gate(send_f, m_in), got_b))
    got_f = ring_exchange(send_f).reshape(2 * slots, quarter)

    pre, piece = (2 * slots, 2 * hidden), (2 * slots, hidden)
    far_b = swap(got_b, CORE)
    grad1, sent_g1 = call(grad_body, [(piece, F32), (piece, BF16)], got_b, far_b, own_out, m_out, flag=flag)
    back_g1 = swap(sent_g1, PAIR)
    act_b, sent_a = call(act_bwd_body, [(pre, F32), (pre, BF16)], got_b, far_b, *w_in, flag=flag)
    back_a = swap(sent_a, PAIR)
    far_f = swap(got_f, CORE)
    act_f, sent_f = call(act_fwd_body, [(pre, F32), (pre, BF16)], got_f, far_f, *w_in, flag=flag)
    back_f = swap(sent_f, PAIR)
    v_out, sent_f, sent_a, back_g1 = lax.optimization_barrier((v_out, sent_f, sent_a, back_g1))
    grad2, sent_g2 = call(grad_body, [(piece, F32), (piece, BF16)], got_b, far_b, m_out, v_out, flag=flag)
    back_g2 = swap(sent_g2, PAIR)
    own, cross = call(
        out_body,
        [((2 * slots, features), F32), ((2 * slots, features), BF16)],
        *(act_f, back_f, act_b, back_a, grad1, back_g1, grad2, back_g2, *w_in, *w_out),
        flag=flag,
    )
    shape = (2 * slots, quarter)
    ret_f, ret_b = call(finish_body, [(shape, BF16), (shape, BF16)], own, swap(cross, CORE), got_b)
    next_b, next_routes = from_behind(ret_b, -1), from_behind(routes_b, -1)
    home_f = ring_exchange(ret_f)
    next_b = gate(next_b)
    (y,) = call(merge_fwd_body, [((tokens, 2 * features), BF16)], routes_f, probs_f, rows_f, home_f)
    home_b = ring_exchange(next_b)
    (dx,) = call(merge_bwd_body, [((tokens, 2 * features), BF16)], next_routes, home_b)
    return from_behind(y[None], 1), dx[None]


def solution(mesh):
    row = P("pipe", "expert", None)
    block = P("pipe", "expert", None, None)
    return jax.shard_map(
        local,
        mesh=mesh,
        in_specs=(row,) * 7 + (block,) * 2,
        out_specs=(row, row),
        check_vma=False,
    )
```

```python
import jax
import jax.numpy as jnp
from jax import lax
from jax.experimental import pallas as pl
from jax.experimental.pallas import tpu as pltpu
from jax.sharding import PartitionSpec as P

EXPERTS = 4
CAP = 20
LANES = 128
F32 = jnp.float32
BF16 = jnp.bfloat16
NN = (((1,), (0,)), ((), ()))
NT = (((1,), (1,)), ((), ()))
TN = (((0,), (0,)), ((), ()))
CORE, PLANE, PAIR = 1, 2, 4
LIMIT = 32 * 1024 * 1024


def dot(left, right, dims=NN):
    return lax.dot_general(left, right, dims, preferred_element_type=F32)


def swap(value, mask, other=None):
    count = lax.axis_size("expert")
    masks = [mask if other is None or keeps(i) else other for i in range(count)]
    return lax.ppermute(value, "expert", [(i, i ^ m) for i, m in enumerate(masks) if m])


def keeps(index):
    return (index >> 2 & 1) == (index & 1)


def from_behind(value, steps):
    count = lax.axis_size("pipe")
    return lax.ppermute(value, "pipe", [(i, (i + steps) % count) for i in range(count)])


def ring_exchange(value):
    count = lax.axis_size("expert")
    rings = count // 4
    groups = [[z * 4 + b for z in range(rings)] for b in range(4)]
    cut = value.reshape(rings, -1, value.shape[-1])
    got = lax.all_to_all(cut, "expert", split_axis=0, concat_axis=0, tiled=True, axis_index_groups=groups)
    return got.reshape(value.shape)


def call(body, outs, *args, after=(), flag=None):
    shapes = [jax.ShapeDtypeStruct(s, d) for s, d in outs]
    flags = () if flag is None else (flag,)
    lead = [pl.BlockSpec(memory_space=pltpu.SMEM) for _ in flags]
    lead += [pl.BlockSpec(memory_space=pl.ANY) for _ in after]

    def run(*refs):
        body(*refs[: len(flags)], *refs[len(flags) + len(after) :])

    args = (*flags, *after, *args)
    return pl.pallas_call(
        run,
        out_shape=shapes,
        in_specs=lead + [pl.BlockSpec(memory_space=pltpu.VMEM) for _ in args[len(lead) :]],
        out_specs=[pl.BlockSpec(memory_space=pltpu.VMEM) for _ in outs],
        compiler_params=pltpu.CompilerParams(vmem_limit_bytes=LIMIT),
    )(*args)


def gate(held, *after):
    return pl.pallas_call(
        lambda *refs: None,
        out_shape=jax.ShapeDtypeStruct(held.shape, held.dtype),
        in_specs=[pl.BlockSpec(memory_space=pl.ANY) for _ in (held, *after)],
        out_specs=pl.BlockSpec(memory_space=pl.ANY),
        input_output_aliases={0: 0},
        cost_estimate=pl.CostEstimate(flops=10**11, bytes_accessed=10**9, transcendentals=0),
    )(held, *after)


def senders(routes, expert):
    count = routes.shape[1]
    mine = jnp.broadcast_to(routes == expert, (2 * CAP, count))
    upto = lax.broadcasted_iota(jnp.int32, (count, count), 0) <= lax.broadcasted_iota(jnp.int32, (count, count), 1)
    rank = dot(mine.astype(F32).astype(BF16), upto.astype(F32).astype(BF16)).astype(jnp.int32) - 1
    row = lax.broadcasted_iota(jnp.int32, (2 * CAP, count), 0)
    low = mine & (rank == row)
    high = mine & (rank == row - CAP)
    return low.astype(F32).astype(BF16), high.astype(F32).astype(BF16)


def pack_fwd_body(routes, rows, out):
    wide = out.shape[2]
    for e in range(EXPERTS):
        low, high = senders(routes[...], e)
        for h in range(2):
            first, second = pl.ds(2 * h * wide, wide), pl.ds((2 * h + 1) * wide, wide)
            out[2 * e + h] = (dot(low, rows[:, first]) + dot(high, rows[:, second])).astype(BF16)


def pack_bwd_body(routes, probs, rows, cots, out):
    wide = out.shape[2] - LANES
    lane = lax.broadcasted_iota(jnp.int32, (rows.shape[0], LANES), 1)
    rest = jnp.broadcast_to(probs[...], lane.shape)
    weight = jnp.zeros(lane.shape, F32)
    for k in range(3):
        part = rest.astype(BF16).astype(F32)
        weight = jnp.where(lane == k, part, weight)
        rest = rest - part
    weight = weight.astype(BF16)
    for e in range(EXPERTS):
        low, high = senders(routes[...], e)
        tail = dot(low, weight).astype(BF16)
        for h in range(2):
            at = pl.ds(h * wide, wide)
            out[2 * e + h, :, pl.ds(0, wide)] = (dot(low, rows[:, at]) + dot(high, cots[:, at])).astype(BF16)
            out[2 * e + h, :, pl.ds(wide, LANES)] = tail


def halves(rows):
    row = lax.broadcasted_iota(jnp.int32, (rows // 2, rows), 0)
    col = lax.broadcasted_iota(jnp.int32, (rows // 2, rows), 1)
    block = row // CAP
    low = col == row + block * CAP
    high = col == row + block * CAP + CAP
    return low.astype(F32).astype(BF16), high.astype(F32).astype(BF16)


def choose(flag, body, *weights):
    keep = flag[0] == 1
    pl.when(keep)(lambda: body(*[w[:-1] for w in weights]))
    pl.when(jnp.logical_not(keep))(lambda: body(*[w[1:] for w in weights]))


def act_fwd_body(flag, own, other, *refs):
    *w_in, act, sent = refs
    rows, wide = own.shape
    low, high = halves(rows)

    def run(pieces):
        for k, ref in enumerate((own, other)):
            a = dot(low, ref[...]).astype(BF16)
            b = dot(high, ref[...]).astype(BF16)
            at = pl.ds(k * (rows // 2), rows // 2)
            for q, w in enumerate(pieces):
                n = w.shape[1]
                part = dot(a, w[pl.ds(0, wide), :]) + dot(b, w[pl.ds(wide, wide), :])
                act[at, pl.ds(q * n, n)] = part
                sent[at, pl.ds(q * n, n)] = part.astype(BF16)

    choose(flag, run, w_in)


def first_bwd_body(flag, own, other, *refs):
    w_in, w_out = refs[:3], refs[3:5]
    act, grad, sent = refs[5:]
    low, high = halves(own.shape[0])
    many = low.shape[0]

    def run(ins, outs):
        (wo,) = outs
        n, wide = wo.shape
        for k, ref in enumerate((own, other)):
            at = pl.ds(k * many, many)
            v = dot(low, ref[:, :wide]).astype(BF16)
            c = dot(high, ref[:, :wide]).astype(BF16)
            for q, w in enumerate(ins):
                part = dot(v, w[...])
                act[at, pl.ds(q * n, n)] = part
                sent[at, pl.ds(q * n, n)] = part.astype(BF16)
            part = dot(c, wo[...], NT)
            grad[at, :] = part
            sent[at, pl.ds(2 * n, n)] = part.astype(BF16)

    choose(flag, run, w_in, w_out)


def grad_body(flag, own, other, *refs):
    *w_out, grad, sent = refs
    _, high = halves(own.shape[0])
    many = high.shape[0]

    def run(pieces):
        for k, ref in enumerate((own, other)):
            c = dot(high, ref[:, : pieces[0].shape[1]]).astype(BF16)
            for q, w in enumerate(pieces):
                at = (pl.ds(k * many, many), pl.ds(q * w.shape[0], w.shape[0]))
                part = dot(c, w[...], NT)
                grad[at] = part
                sent[at] = part.astype(BF16)

    choose(flag, run, w_out)


def out_body(flag, act_f, got_f, act_b, grad1, got_b, grad2, got_grad2, *refs):
    w_in, w_out = refs[:3], refs[3:6]
    own, sent = refs[6:]
    n = grad1.shape[1]
    half = own.shape[0] // 2
    a = act_f[...] + got_f[...].astype(F32)
    h = (a * jax.nn.sigmoid(a)).astype(BF16)
    r = []
    for q, (grad, got) in enumerate(((grad1, got_b[:, pl.ds(2 * n, n)]), (grad2, got_grad2[...]))):
        at = pl.ds(q * n, n)
        a = act_b[:, at] + got_b[:, at].astype(F32)
        g = grad[...] + got.astype(F32)
        s = jax.nn.sigmoid(a)
        r.append((g * s * (1.0 + a * (1.0 - s))).astype(BF16))

    def run(ins, outs):
        o = dot(h[:, :n], outs[0][...]) + dot(h[:, n:], outs[1][...])
        u = dot(r[0], ins[0][...], NT) + dot(r[1], ins[1][...], NT)
        for k, part in enumerate((o, u)):
            at = pl.ds(k * half, half)
            own[at, :] = part[:half]
            sent[at, :] = part[half:].astype(BF16)

    choose(flag, run, w_in, w_out)


def finish_body(own, got, sent, out_f, out_b):
    low, high = halves(out_f.shape[0])
    wide = out_f.shape[1]
    half = own.shape[0] // 2
    total = own[...] + got[...].astype(F32)
    weight = jnp.sum(dot(low, sent[:, 2 * wide :]), axis=1, keepdims=True)
    ready = (dot(high, sent[:, : 2 * wide]) + weight * total[half:]).astype(BF16)
    for rows, out in ((total[:half].astype(BF16), out_f), (ready, out_b)):
        out[...] = (dot(low, rows[:, :wide], TN) + dot(high, rows[:, wide:], TN)).astype(BF16)


def homing(routes, got, place):
    wide = got.shape[1]
    block = 2 * CAP
    picks = [senders(routes[...], e) for e in range(EXPERTS)]
    for h in range(2):
        for q in range(2):
            total = None
            for e in range(EXPERTS):
                part = dot(picks[e][q], got[pl.ds((2 * e + h) * block, block), :], TN)
                total = part if total is None else total + part
            place(pl.ds((2 * h + q) * wide, wide), total)


def merge_fwd_body(routes, probs, rows, got, out):
    def place(at, total):
        out[:, at] = (rows[:, at].astype(F32) + probs[...] * total).astype(BF16)

    homing(routes, got, place)


def merge_bwd_body(routes, got, out):
    def place(at, total):
        out[:, at] = total.astype(BF16)

    homing(routes, got, place)


def local(
    fwd_tokens,
    bwd_tokens,
    bwd_cotangent,
    fwd_routes,
    bwd_routes,
    fwd_probs,
    bwd_probs,
    expert_in,
    expert_out,
):
    rings = lax.axis_size("expert") // 4
    index = lax.axis_index("expert")
    keep = (index >> 2 & 1) == (index & 1)
    own_in, own_out = expert_in[0, 0], expert_out[0, 0]
    features, hidden = own_in.shape
    quarter = features // 2
    slots = rings * CAP
    tokens = fwd_tokens.shape[1]
    rows_f, rows_b, rows_c = fwd_tokens[0], bwd_tokens[0], bwd_cotangent[0]
    routes_f, routes_b = fwd_routes.reshape(1, tokens), bwd_routes.reshape(1, tokens)
    probs_f, probs_b = fwd_probs.reshape(tokens, 1), bwd_probs.reshape(tokens, 1)

    m_in = swap(own_in, PLANE, PAIR | CORE)
    m_out = swap(own_out, PLANE, PAIR | CORE)
    v_in = swap(m_in, 0, PLANE)
    early_out, v_in = lax.optimization_barrier((m_out, v_in))
    v_out = swap(early_out, 0, PLANE)
    w_in, w_out = (own_in, m_in, v_in), (own_out, m_out, v_out)
    flag = keep.astype(jnp.int32).reshape(1)

    (send_f,) = call(pack_fwd_body, [((2 * EXPERTS, 2 * CAP, quarter), BF16)], routes_f, rows_f)
    (send_b,) = call(
        pack_bwd_body, [((2 * EXPERTS, 2 * CAP, features + LANES), BF16)], routes_b, probs_b, rows_b, rows_c
    )
    got_b = ring_exchange(send_b).reshape(2 * slots, features + LANES)
    send_f, got_b = lax.optimization_barrier((gate(send_f, m_in), got_b))
    got_f = ring_exchange(send_f).reshape(2 * slots, quarter)

    pre, piece = (2 * slots, 2 * hidden), (2 * slots, hidden)
    far_b = swap(got_b, CORE)
    act_b, grad1, sent_b = call(
        first_bwd_body,
        [(pre, F32), (piece, F32), ((2 * slots, 3 * hidden), BF16)],
        *(got_b, far_b, *w_in, own_out, m_out),
        flag=flag,
    )
    back_b = swap(sent_b, PAIR)
    far_f = swap(got_f, CORE)
    act_f, sent_f = call(act_fwd_body, [(pre, F32), (pre, BF16)], got_f, far_f, *w_in, flag=flag)
    back_f = swap(sent_f, PAIR)
    v_out, sent_f, sent_b = lax.optimization_barrier((v_out, sent_f, sent_b))
    grad2, sent_g2 = call(grad_body, [(piece, F32), (piece, BF16)], got_b, far_b, m_out, v_out, flag=flag)
    back_g2 = swap(sent_g2, PAIR)
    own, cross = call(
        out_body,
        [((2 * slots, features), F32), ((2 * slots, features), BF16)],
        *(act_f, back_f, act_b, grad1, back_b, grad2, back_g2, *w_in, *w_out),
        flag=flag,
    )
    shape = (2 * slots, quarter)
    ret_f, ret_b = call(finish_body, [(shape, BF16), (shape, BF16)], own, swap(cross, CORE), got_b)
    next_b, next_routes = from_behind(ret_b, -1), from_behind(routes_b, -1)
    home_f = ring_exchange(ret_f)
    next_b = gate(next_b)
    (y,) = call(merge_fwd_body, [((tokens, 2 * features), BF16)], routes_f, probs_f, rows_f, home_f)
    home_b = ring_exchange(next_b)
    (dx,) = call(merge_bwd_body, [((tokens, 2 * features), BF16)], next_routes, home_b)
    return from_behind(y[None], 1), dx[None]


def solution(mesh):
    row = P("pipe", "expert", None)
    block = P("pipe", "expert", None, None)
    return jax.shard_map(
        local,
        mesh=mesh,
        in_specs=(row,) * 7 + (block,) * 2,
        out_specs=(row, row),
        check_vma=False,
    )
```

```python
import jax
import jax.numpy as jnp
from jax import lax
from jax.experimental import pallas as pl
from jax.experimental.pallas import tpu as pltpu
from jax.sharding import PartitionSpec as P

EXPERTS = 4
CAP = 20
LANES = 128
F32 = jnp.float32
BF16 = jnp.bfloat16
NN = (((1,), (0,)), ((), ()))
NT = (((1,), (1,)), ((), ()))
TN = (((0,), (0,)), ((), ()))
CORE, PLANE, PAIR = 1, 2, 4
LIMIT = 32 * 1024 * 1024


def dot(left, right, dims=NN):
    return lax.dot_general(left, right, dims, preferred_element_type=F32)


def swap(value, mask, other=None):
    count = lax.axis_size("expert")
    masks = [mask if other is None or keeps(i) else other for i in range(count)]
    return lax.ppermute(value, "expert", [(i, i ^ m) for i, m in enumerate(masks) if m])


def keeps(index):
    return (index >> 2 & 1) == (index & 1)


def from_behind(value, steps):
    count = lax.axis_size("pipe")
    return lax.ppermute(value, "pipe", [(i, (i + steps) % count) for i in range(count)])


def ring_exchange(value):
    count = lax.axis_size("expert")
    rings = count // 4
    groups = [[z * 4 + b for z in range(rings)] for b in range(4)]
    cut = value.reshape(rings, -1, value.shape[-1])
    got = lax.all_to_all(cut, "expert", split_axis=0, concat_axis=0, tiled=True, axis_index_groups=groups)
    return got.reshape(value.shape)


def call(body, outs, *args, after=(), flag=None):
    shapes = [jax.ShapeDtypeStruct(s, d) for s, d in outs]
    flags = () if flag is None else (flag,)
    lead = [pl.BlockSpec(memory_space=pltpu.SMEM) for _ in flags]
    lead += [pl.BlockSpec(memory_space=pl.ANY) for _ in after]

    def run(*refs):
        body(*refs[: len(flags)], *refs[len(flags) + len(after) :])

    args = (*flags, *after, *args)
    return pl.pallas_call(
        run,
        out_shape=shapes,
        in_specs=lead + [pl.BlockSpec(memory_space=pltpu.VMEM) for _ in args[len(lead) :]],
        out_specs=[pl.BlockSpec(memory_space=pltpu.VMEM) for _ in outs],
        compiler_params=pltpu.CompilerParams(vmem_limit_bytes=LIMIT),
    )(*args)


def gate(held, *after):
    return pl.pallas_call(
        lambda *refs: None,
        out_shape=jax.ShapeDtypeStruct(held.shape, held.dtype),
        in_specs=[pl.BlockSpec(memory_space=pl.ANY) for _ in (held, *after)],
        out_specs=pl.BlockSpec(memory_space=pl.ANY),
        input_output_aliases={0: 0},
        cost_estimate=pl.CostEstimate(flops=10**11, bytes_accessed=10**9, transcendentals=0),
    )(held, *after)


def senders(routes, expert):
    count = routes.shape[1]
    mine = jnp.broadcast_to(routes == expert, (2 * CAP, count))
    upto = lax.broadcasted_iota(jnp.int32, (count, count), 0) <= lax.broadcasted_iota(jnp.int32, (count, count), 1)
    rank = dot(mine.astype(F32).astype(BF16), upto.astype(F32).astype(BF16)).astype(jnp.int32) - 1
    row = lax.broadcasted_iota(jnp.int32, (2 * CAP, count), 0)
    low = mine & (rank == row)
    high = mine & (rank == row - CAP)
    return low.astype(F32).astype(BF16), high.astype(F32).astype(BF16)


def pack_fwd_body(routes, rows, out):
    wide = out.shape[2]
    for e in range(EXPERTS):
        low, high = senders(routes[...], e)
        for h in range(2):
            first, second = pl.ds(2 * h * wide, wide), pl.ds((2 * h + 1) * wide, wide)
            out[2 * e + h] = (dot(low, rows[:, first]) + dot(high, rows[:, second])).astype(BF16)


def pack_bwd_body(routes, probs, rows, cots, out):
    wide = out.shape[2] - LANES
    lane = lax.broadcasted_iota(jnp.int32, (rows.shape[0], LANES), 1)
    rest = jnp.broadcast_to(probs[...], lane.shape)
    weight = jnp.zeros(lane.shape, F32)
    for k in range(3):
        part = rest.astype(BF16).astype(F32)
        weight = jnp.where(lane == k, part, weight)
        rest = rest - part
    weight = weight.astype(BF16)
    for e in range(EXPERTS):
        low, high = senders(routes[...], e)
        tail = dot(low, weight).astype(BF16)
        for h in range(2):
            at = pl.ds(h * wide, wide)
            out[2 * e + h, :, pl.ds(0, wide)] = (dot(low, rows[:, at]) + dot(high, cots[:, at])).astype(BF16)
            out[2 * e + h, :, pl.ds(wide, LANES)] = tail


def halves(rows):
    row = lax.broadcasted_iota(jnp.int32, (rows // 2, rows), 0)
    col = lax.broadcasted_iota(jnp.int32, (rows // 2, rows), 1)
    block = row // CAP
    low = col == row + block * CAP
    high = col == row + block * CAP + CAP
    return low.astype(F32).astype(BF16), high.astype(F32).astype(BF16)


def choose(flag, body, *weights):
    keep = flag[0] == 1
    pl.when(keep)(lambda: body(*[w[:-1] for w in weights]))
    pl.when(jnp.logical_not(keep))(lambda: body(*[w[1:] for w in weights]))


def act_fwd_body(flag, own, other, *refs):
    *w_in, act, sent = refs
    rows, wide = own.shape
    low, high = halves(rows)

    def run(pieces):
        for k, ref in enumerate((own, other)):
            a = dot(low, ref[...]).astype(BF16)
            b = dot(high, ref[...]).astype(BF16)
            at = pl.ds(k * (rows // 2), rows // 2)
            for q, w in enumerate(pieces):
                n = w.shape[1]
                part = dot(a, w[pl.ds(0, wide), :]) + dot(b, w[pl.ds(wide, wide), :])
                act[at, pl.ds(q * n, n)] = part
                sent[at, pl.ds(q * n, n)] = part.astype(BF16)

    choose(flag, run, w_in)


def act_bwd_body(flag, own, other, *refs):
    *w_in, act, sent = refs
    low, _ = halves(own.shape[0])
    many = low.shape[0]

    def run(pieces):
        for k, ref in enumerate((own, other)):
            v = dot(low, ref[:, : pieces[0].shape[0]]).astype(BF16)
            for q, w in enumerate(pieces):
                at = (pl.ds(k * many, many), pl.ds(q * w.shape[1], w.shape[1]))
                part = dot(v, w[...])
                act[at] = part
                sent[at] = part.astype(BF16)

    choose(flag, run, w_in)


def grad_body(flag, own, other, *refs):
    *w_out, grad, sent = refs
    _, high = halves(own.shape[0])
    many = high.shape[0]

    def run(pieces):
        for k, ref in enumerate((own, other)):
            c = dot(high, ref[:, : pieces[0].shape[1]]).astype(BF16)
            for q, w in enumerate(pieces):
                at = (pl.ds(k * many, many), pl.ds(q * w.shape[0], w.shape[0]))
                part = dot(c, w[...], NT)
                grad[at] = part
                sent[at] = part.astype(BF16)

    choose(flag, run, w_out)


def out_body(flag, act_f, got_f, act_b, got_b, grad1, got_grad1, grad2, got_grad2, *refs):
    w_in, w_out = refs[:3], refs[3:6]
    own, sent = refs[6:]
    n = grad1.shape[1]
    half = own.shape[0] // 2
    a = act_f[...] + got_f[...].astype(F32)
    h = (a * jax.nn.sigmoid(a)).astype(BF16)
    r = []
    for q, (grad, got) in enumerate(((grad1, got_grad1), (grad2, got_grad2))):
        at = pl.ds(q * n, n)
        a = act_b[:, at] + got_b[:, at].astype(F32)
        g = grad[...] + got[...].astype(F32)
        s = jax.nn.sigmoid(a)
        r.append((g * s * (1.0 + a * (1.0 - s))).astype(BF16))

    def run(ins, outs):
        o = dot(h[:, :n], outs[0][...]) + dot(h[:, n:], outs[1][...])
        u = dot(r[0], ins[0][...], NT) + dot(r[1], ins[1][...], NT)
        for k, part in enumerate((o, u)):
            at = pl.ds(k * half, half)
            own[at, :] = part[:half]
            sent[at, :] = part[half:].astype(BF16)

    choose(flag, run, w_in, w_out)


def finish_body(own, got, sent, out_f, out_b):
    low, high = halves(out_f.shape[0])
    wide = out_f.shape[1]
    half = own.shape[0] // 2
    total = own[...] + got[...].astype(F32)
    weight = jnp.sum(dot(low, sent[:, 2 * wide :]), axis=1, keepdims=True)
    ready = (dot(high, sent[:, : 2 * wide]) + weight * total[half:]).astype(BF16)
    for rows, out in ((total[:half].astype(BF16), out_f), (ready, out_b)):
        out[...] = (dot(low, rows[:, :wide], TN) + dot(high, rows[:, wide:], TN)).astype(BF16)


def homing(routes, got, place):
    wide = got.shape[1]
    block = 2 * CAP
    picks = [senders(routes[...], e) for e in range(EXPERTS)]
    for h in range(2):
        for q in range(2):
            total = None
            for e in range(EXPERTS):
                part = dot(picks[e][q], got[pl.ds((2 * e + h) * block, block), :], TN)
                total = part if total is None else total + part
            place(pl.ds((2 * h + q) * wide, wide), total)


def merge_fwd_body(routes, probs, rows, got, out):
    def place(at, total):
        out[:, at] = (rows[:, at].astype(F32) + probs[...] * total).astype(BF16)

    homing(routes, got, place)


def merge_bwd_body(routes, got, out):
    def place(at, total):
        out[:, at] = total.astype(BF16)

    homing(routes, got, place)


def local(
    fwd_tokens,
    bwd_tokens,
    bwd_cotangent,
    fwd_routes,
    bwd_routes,
    fwd_probs,
    bwd_probs,
    expert_in,
    expert_out,
):
    rings = lax.axis_size("expert") // 4
    index = lax.axis_index("expert")
    keep = (index >> 2 & 1) == (index & 1)
    own_in, own_out = expert_in[0, 0], expert_out[0, 0]
    features, hidden = own_in.shape
    quarter = features // 2
    slots = rings * CAP
    tokens = fwd_tokens.shape[1]
    rows_f, rows_b, rows_c = fwd_tokens[0], bwd_tokens[0], bwd_cotangent[0]
    routes_f, routes_b = fwd_routes.reshape(1, tokens), bwd_routes.reshape(1, tokens)
    probs_f, probs_b = fwd_probs.reshape(tokens, 1), bwd_probs.reshape(tokens, 1)

    m_in = swap(own_in, PLANE, PAIR | CORE)
    m_out = swap(own_out, PLANE, PAIR | CORE)
    v_in = swap(m_in, 0, PLANE)
    early_out, v_in = lax.optimization_barrier((m_out, v_in))
    v_out = swap(early_out, 0, PLANE)
    w_in, w_out = (own_in, m_in, v_in), (own_out, m_out, v_out)
    flag = keep.astype(jnp.int32).reshape(1)

    (send_f,) = call(pack_fwd_body, [((2 * EXPERTS, 2 * CAP, quarter), BF16)], routes_f, rows_f)
    (send_b,) = call(
        pack_bwd_body, [((2 * EXPERTS, 2 * CAP, features + LANES), BF16)], routes_b, probs_b, rows_b, rows_c
    )
    got_b = ring_exchange(send_b).reshape(2 * slots, features + LANES)
    send_f, got_b = lax.optimization_barrier((gate(send_f, m_in), got_b))
    got_f = ring_exchange(send_f).reshape(2 * slots, quarter)

    pre, piece = (2 * slots, 2 * hidden), (2 * slots, hidden)
    far_b = swap(got_b, CORE)
    grad1, sent_g1 = call(grad_body, [(piece, F32), (piece, BF16)], got_b, far_b, own_out, m_out, flag=flag)
    back_g1 = swap(sent_g1, PAIR)
    act_b, sent_a = call(act_bwd_body, [(pre, F32), (pre, BF16)], got_b, far_b, *w_in, flag=flag)
    back_a = swap(sent_a, PAIR)
    far_f = swap(got_f, CORE)
    act_f, sent_f = call(act_fwd_body, [(pre, F32), (pre, BF16)], got_f, far_f, *w_in, flag=flag)
    back_f = swap(sent_f, PAIR)
    v_out, sent_f, sent_a, back_g1 = lax.optimization_barrier((v_out, sent_f, sent_a, back_g1))
    grad2, sent_g2 = call(grad_body, [(piece, F32), (piece, BF16)], got_b, far_b, m_out, v_out, flag=flag)
    back_g2 = swap(sent_g2, PAIR)
    own, cross = call(
        out_body,
        [((2 * slots, features), F32), ((2 * slots, features), BF16)],
        *(act_f, back_f, act_b, back_a, grad1, back_g1, grad2, back_g2, *w_in, *w_out),
        flag=flag,
    )
    shape = (2 * slots, quarter)
    ret_f, ret_b = call(finish_body, [(shape, BF16), (shape, BF16)], own, swap(cross, CORE), got_b)
    next_b, next_routes = from_behind(ret_b, -1), from_behind(routes_b, -1)
    home_f = ring_exchange(ret_f)
    next_b = gate(next_b)
    (y,) = call(merge_fwd_body, [((tokens, 2 * features), BF16)], routes_f, probs_f, rows_f, home_f)
    home_b = ring_exchange(next_b)
    passed = from_behind(y[None], 1)
    dx, passed = pl.pallas_call(
        lambda routes, got, _, out, __: merge_bwd_body(routes, got, out),
        out_shape=[jax.ShapeDtypeStruct((tokens, 2 * features), BF16), jax.ShapeDtypeStruct(passed.shape, BF16)],
        in_specs=[pl.BlockSpec(memory_space=m) for m in (pltpu.VMEM, pltpu.VMEM, pl.ANY)],
        out_specs=[pl.BlockSpec(memory_space=m) for m in (pltpu.VMEM, pl.ANY)],
        input_output_aliases={2: 1},
        compiler_params=pltpu.CompilerParams(vmem_limit_bytes=LIMIT),
    )(next_routes, home_b, passed)
    return passed, dx[None]


def solution(mesh):
    row = P("pipe", "expert", None)
    block = P("pipe", "expert", None, None)
    return jax.shard_map(
        local,
        mesh=mesh,
        in_specs=(row,) * 7 + (block,) * 2,
        out_specs=(row, row),
        check_vma=False,
    )
```
